128 devices in a mesh: tm: 4 (over z), tile: 32 (over x, y, core).
Axes of the slice: x: 4, y: 4, z: 4, core: 2. Of those that a mesh axis runs over, the one named last changes fastest.
Arguments:
- multiplier: float32 [4, 4, 1536, 1536], P('tm', None, 'tile'), may hold values from -7 to 7
- obs_dual: float32 [4, 4096], P('tm', 'tile'), may hold values from -6 to 6
- increment: float32 [4, 4, 1536, 1536], P('tm', None, 'tile'), may hold values from -6 to 6
- error_var: float32 [4, 4, 1536, 1536], P('tm', None, 'tile'), may hold values from 0.3 to 3
- obs_var: float32 [4, 4096], P('tm', 'tile'), may hold values from 0.1 to 1
- winds: bfloat16 [4, 2, 4, 1536, 1536], P('tm', None, None, 'tile'), may hold values from -0.29882812 to 0.29882812
- wake_mask: int32 [1536, 1536], P('tile'), may hold values 0 or 1
- obs_cell: int32 [4, 4096], P('tm', 'tile'), may hold values from 0 to 294911
Outputs:
- out_multiplier: float32 [4, 4, 1536, 1536], P('tm', None, 'tile')
- out_obs: float32 [4, 4096], P('tm', 'tile')
- out_increment: float32 [4, 4, 1536, 1536], P('tm', None, 'tile')
- curvature: float32 [], replicated
The draws below stay inside these ranges and needn't reach their ends.
Inputs may be any that keep to these rules, and one draw needn't show every extreme that they name: `obs_cell`: entries of block j // 128 name a cell of strip j // 128, as (level 48 + row) * 1536 + column with the row counted within the strip; several observations may share a cell.
All inputs are finite; a program needn't handle non-finite values. No bound on the sum of `wake_mask` on one device may be relied on, other than what follows from the above.
Results may differ from the reference program's by a relative error of at most 0.0003.
Values sent between devices are 32-bit elements; how exact they have to be, the bound alone decides.
No kernel may reach another device: no remote copies, remote signals or barrier semaphores. Data moves between devices by JAX's collectives and lax.ppermute only.
A program may use at most 128 MiB of HBM per device.

```python
import math
import jax
import jax.numpy as jnp

LEV = 4
ROWS_DEV = 48
NY = 1536
SUB = 6
OBS_DEV = 128
SUBWIN = 4
NX = 1536
NOBS = 4096


def layered(key, count, amp_lo, amp_hi):
    amp_key, sign_key, normal_key = jax.random.split(key, 3)
    amplitude = jax.random.uniform(amp_key, (count, LEV, 1, 1), jnp.float32, amp_lo, amp_hi)
    signs = 2.0 * jax.random.bernoulli(sign_key, 0.5, (count, LEV, 1, 1)).astype(jnp.float32) - 1.0
    rough = jnp.clip(jax.random.normal(normal_key, (count, LEV, NX, NY), jnp.float32), -3.5, 3.5)
    return amplitude * signs + rough


def draw_increment(key, part):
    common = layered(key, SUBWIN, 1.5, 2.5)
    return common.astype(jnp.float32)


def draw_multiplier(key, part):
    common = layered(key, SUBWIN, 1.5, 2.5)
    key = jax.random.fold_in(key, 5)
    first_key, own_key = jax.random.split(key)
    first = layered(first_key, 1, 1.5, 2.5)
    own = layered(own_key, SUBWIN, 0.0, 0.0)
    leading = 0.8 * first + 0.6 * own[:1]
    later = 0.8 * common[:-1] + 0.6 * own[1:]
    return jnp.concatenate([leading, later], axis=0).astype(jnp.float32)


def touch_ends(result, rng, low, largest):
    longest = result.shape.index(max(result.shape))
    spots = []
    for shift in (0, 1):
        where = [jax.random.randint(jax.random.fold_in(rng, axis), (), 0, length) for axis, length in enumerate(result.shape)]
        where[longest] = (where[longest] + shift) % result.shape[longest]
        spots.append(tuple(where))
    return result.at[spots[0]].set(low).at[spots[1]].set(largest)


def steps_of(key, shape, cuts, smallest, largest):
    def one(position, blocks):
        heights = jax.random.uniform(jax.random.fold_in(jax.random.fold_in(key, 6), position), (blocks,), jnp.float32, smallest / len(cuts), largest / len(cuts))
        return jnp.repeat(jnp.exp(heights), shape[position] // blocks).reshape((-1,) + (1,) * (len(shape) - position - 1))

    level = one(*cuts[0])
    for cut in cuts[1:]:
        level = level * one(*cut)
    return level


def noise(rng, shape, scale, limit, cuts=(), dtype=jnp.bfloat16):
    gain = steps_of(rng, shape, cuts, -0.22, 0.18) if cuts else 1.0
    drawn = jax.random.normal(rng, shape, jnp.float32) * scale * gain
    return jnp.minimum(jnp.maximum(drawn, -limit), limit).astype(dtype)


def setup_inputs(seed: int = 0) -> dict:
    keys = jax.random.split(jax.random.key(seed), 9)
    return {
        "multiplier": draw_multiplier(jax.random.fold_in(keys[8], 71), 0),
        "obs_dual": noise(keys[1], (SUBWIN, NOBS), 1.0, 6.0, ((0, 4), (1, 32)), jnp.float32),
        "increment": draw_increment(jax.random.fold_in(keys[8], 71), 0),
        "error_var": jnp.clip(jnp.exp(math.log(3.0) - 2.3025851 * jax.random.uniform(keys[3], (SUBWIN, LEV, NX, NY), jnp.float32) ** steps_of(keys[3], (SUBWIN, LEV, NX, NY), ((0, 4), (2, 32)), -0.2, 0.2)), 0.3, 3.0),
        "obs_var": jnp.clip(jnp.exp(math.log(1.0) - 2.3025851 * jax.random.uniform(keys[4], (SUBWIN, NOBS), jnp.float32) ** steps_of(keys[4], (SUBWIN, NOBS), ((0, 4), (1, 32)), -0.2, 0.2)), 0.1, 1.0),
        "winds": jnp.clip(jax.random.uniform(keys[5], (SUBWIN, 2, LEV, NX, NY), jnp.float32, -0.29882812, 0.29882812) * steps_of(keys[5], (SUBWIN, 2, LEV, NX, NY), ((0, 4), (3, 32)), -0.4, 0.0), -0.29882812, 0.29882812).astype(jnp.bfloat16),
        "wake_mask": touch_ends((jax.random.randint(keys[6], (NX, NY), 0, 4) < 1).astype(jnp.int32), jax.random.fold_in(keys[6], 1), 0, 1),
        "obs_cell": touch_ends(jax.random.randint(keys[7], (SUBWIN, NOBS), 0, LEV * ROWS_DEV * NY), jax.random.fold_in(keys[7], 1), 0, (LEV * ROWS_DEV * NY) - 1).astype(jnp.int32),
    }


kappa_base = 0.04
vertical_mix = 0.05

def coefficients(wind, wake):
    speed_x = wind[0].astype(jnp.float32)
    speed_y = wind[1].astype(jnp.float32)
    diffusion = jnp.broadcast_to(kappa_base * (1.0 + 2.0 * wake.astype(jnp.float32)), speed_x.shape)
    return jnp.stack([jnp.maximum(speed_x, 0.0), jnp.minimum(speed_x, 0.0), jnp.maximum(speed_y, 0.0), jnp.minimum(speed_y, 0.0), diffusion])

def substep(padded, coeffs):
    middle = padded[:, 1:-1]
    prior = padded[:, :-2]
    later = padded[:, 2:]
    sideways = jnp.pad(middle, ((0, 0), (0, 0), (1, 1)))
    leftward = sideways[:, :, :-2]
    rightward = sideways[:, :, 2:]
    vertical = jnp.pad(middle, ((1, 1), (0, 0), (0, 0)))
    beneath = vertical[:-2]
    overhead = vertical[2:]
    return middle - coeffs[0] * (middle - prior) - coeffs[1] * (later - middle) - coeffs[2] * (middle - leftward) - coeffs[3] * (rightward - middle) + coeffs[4] * (prior + later + leftward + rightward - 4.0 * middle) + vertical_mix * (beneath + overhead - 2.0 * middle)

def model(field, coeffs):
    for section in range(SUB):
        field = substep(jnp.pad(field, ((0, 0), (1, 1), (0, 0))), coeffs)
    return field

def model_adjoint(field, coeffs):
    _, pull = jax.vjp(lambda state: model(state, coeffs), jnp.zeros_like(field))
    return pull(field)[0]

def reference(multiplier, obs_dual, increment, error_var, obs_var, winds, wake_mask, obs_cell):
    strip_of = (jnp.arange(NOBS) // OBS_DEV).astype(jnp.int32)
    level = obs_cell // (ROWS_DEV * NY)
    rest = obs_cell % (ROWS_DEV * NY)
    row_local = rest // NY
    column = rest % NY
    flat_global = (level * (NX * NY) + (strip_of[None, :] * ROWS_DEV + row_local) * NY + column).astype(jnp.int32)
    moved_list = []
    out_mult_list = []
    out_obs_list = []
    out_inc_list = []
    for window in range(SUBWIN):
        coeffs = coefficients(winds[window], wake_mask)
        moved_list.append(model(increment[window], coeffs))
        if window < SUBWIN - 1:
            backward = model_adjoint(multiplier[window + 1], coeffs)
        else:
            backward = jnp.zeros_like(multiplier[window])
        linear_part = increment[window]
        if window > 0:
            linear_part = linear_part - moved_list[window - 1]
        out_mult_list.append(error_var[window] * multiplier[window] + linear_part)
        sampled = increment[window].reshape(-1)[flat_global[window]]
        out_obs_list.append(obs_var[window] * obs_dual[window] + sampled)
        spread = jnp.zeros((LEV * NX * NY,), jnp.float32).at[flat_global[window]].add(obs_dual[window])
        out_inc_list.append(multiplier[window] - backward + spread.reshape(LEV, NX, NY))
    out_multiplier = jnp.stack(out_mult_list)
    out_obs = jnp.stack(out_obs_list)
    out_increment = jnp.stack(out_inc_list)
    total = jnp.sum(multiplier * out_multiplier) + jnp.sum(obs_dual * out_obs) + jnp.sum(increment * out_increment)
    curvature = total / jnp.float32(SUBWIN * (2 * LEV * NX * NY + NOBS))
    return (out_multiplier, out_obs, out_increment, curvature)
```

```python
import functools

import jax
import jax.numpy as jnp
from jax import lax
from jax.experimental import pallas as pl
from jax.experimental.pallas import tpu as pltpu
from jax.sharding import PartitionSpec as P

SUB = 6
LANES = 128
KAPPA = 0.04
MIX = 0.05
BASE = 16
EDGE = 8
INC, WIND, KD, MULT = 0, 4, 12, 13
CHANNELS = 17
MIB = 2**20


def call(body, out_shape, *args, scratch=(), in_specs=None, vmem=48, flops=1000, grid=None):
    kwargs = {}
    if in_specs is not None:
        kwargs["in_specs"] = in_specs
    if grid is not None:
        kwargs["grid"] = grid
    return pl.pallas_call(
        body,
        out_shape=out_shape,
        scratch_shapes=list(scratch),
        compiler_params=pltpu.CompilerParams(vmem_limit_bytes=vmem * MIB),
        cost_estimate=pl.CostEstimate(flops=flops, bytes_accessed=1000, transcendentals=0),
        **kwargs,
    )(*args)


def f32(*shape):
    return jax.ShapeDtypeStruct(shape, jnp.float32)


def cols(j):
    return pl.ds(j * LANES, LANES)


def diffusion_of(wake):
    return KAPPA * (1.0 + 2.0 * wake.astype(jnp.float32))


def put_coeffs(coef, u, v, kd, level, j, row, rows, adjoint):
    north = jnp.maximum(u, 0.0) + kd
    south = kd - jnp.minimum(u, 0.0)
    west = jnp.maximum(v, 0.0) + kd
    east = kd - jnp.minimum(v, 0.0)
    coef[0, level, j, pl.ds(row, rows), :] = (1.0 - 2.0 * MIX) - ((north + south) + (west + east))
    if adjoint:
        coef[1, level, j, pl.ds(row + 1, rows), :] = south
        coef[2, level, j, pl.ds(row - 1, rows), :] = north
        coef[3, level, j, pl.ds(row, rows), :] = east
        coef[4, level, j, pl.ds(row, rows), :] = west
    else:
        coef[1, level, j, pl.ds(row, rows), :] = north
        coef[2, level, j, pl.ds(row, rows), :] = south
        coef[3, level, j, pl.ds(row, rows), :] = west
        coef[4, level, j, pl.ds(row, rows), :] = east


def own_coeffs(coef, winds, wake, tiles, adjoint):
    levels, columns = winds.shape[1], winds.shape[3] // LANES
    for tile in tiles:
        row = tile * 16
        for j in range(columns):
            kd = diffusion_of(wake[pl.ds(row, 16), cols(j)])
            for level in range(levels):
                u = winds[0, level, pl.ds(row, 16), cols(j)].astype(jnp.float32)
                v = winds[1, level, pl.ds(row, 16), cols(j)].astype(jnp.float32)
                put_coeffs(coef, u, v, kd, level, j, BASE + row, 16, adjoint)


def halo_coeffs(coef, halo, row, levels, columns, adjoint):
    for j in range(columns):
        kd = halo[pl.ds(KD * SUB, SUB), cols(j)]
        for level in range(levels):
            u = halo[pl.ds((WIND + level) * SUB, SUB), cols(j)]
            v = halo[pl.ds((WIND + levels + level) * SUB, SUB), cols(j)]
            put_coeffs(coef, u, v, kd, level, j, row, SUB, adjoint)


def substep_tile(src, dst, coef, row, adjoint):
    levels, columns = src.shape[0], src.shape[1]
    lane = lax.broadcasted_iota(jnp.int32, (8, LANES), 1)
    first, last = lane == 0, lane == LANES - 1
    zero = jnp.zeros((8, LANES), jnp.float32)

    def at(k, level, j):
        return coef[k, level, j, pl.ds(row, 8), :]

    def load(j):
        middle = [src[level, j, pl.ds(row, 8), :] for level in range(levels)]
        if adjoint:
            to_east = [at(3, level, j) * middle[level] for level in range(levels)]
            to_west = [at(4, level, j) * middle[level] for level in range(levels)]
        else:
            to_east = to_west = middle
        return (
            middle,
            [pltpu.roll(x, 1, 1) for x in to_east],
            [pltpu.roll(x, LANES - 1, 1) for x in to_west],
        )

    middle, rolled_e, rolled_w = load(0)
    before = [zero] * levels
    for j in range(columns):
        if j + 1 < columns:
            after, after_e, after_w = load(j + 1)
        else:
            after, after_e, after_w = None, None, [zero] * levels
        for level in range(levels):
            west = jnp.where(first, before[level], rolled_e[level])
            east = jnp.where(last, after_w[level], rolled_w[level])
            if not adjoint:
                west = at(3, level, j) * west
                east = at(4, level, j) * east
            total = at(0, level, j) * middle[level]
            total += at(1, level, j) * src[level, j, pl.ds(row - 1, 8), :]
            total += at(2, level, j) * src[level, j, pl.ds(row + 1, 8), :]
            total += west
            total += east
            if level == 0:
                vertical = middle[1]
            elif level == levels - 1:
                vertical = middle[level - 1]
            else:
                vertical = middle[level - 1] + middle[level + 1]
            dst[level, j, pl.ds(row, 8), :] = total + MIX * vertical
        before = rolled_e
        middle, rolled_e, rolled_w = after, after_e, after_w


def run_model(a, b, coef, spans, adjoint):
    for step in range(SUB):
        src, dst = (a, b) if step % 2 == 0 else (b, a)
        reach = SUB - 1 - step
        for low, high in spans:
            start = BASE + low - reach
            tiles = -(-(high - low + 2 * reach) // 8)

            def tile(i, carry, src=src, dst=dst, start=start):
                substep_tile(src, dst, coef, start + i * 8, adjoint)
                return carry

            lax.fori_loop(0, tiles, tile, 0)


def pack_kernel(inc_t, inc_b, mult_t, mult_b, wind_t, wind_b, wake_t, wake_b, top, bottom):
    levels = inc_t.shape[0]
    for out, inc, mult, wind, wake, at in (
        (top, inc_t, mult_t, wind_t, wake_t, 0),
        (bottom, inc_b, mult_b, wind_b, wake_b, 2),
    ):
        for level in range(levels):
            out[pl.ds((INC + level) * SUB, SUB), :] = inc[level, at : at + SUB, :]
            out[pl.ds((MULT + level) * SUB, SUB), :] = mult[level, at : at + SUB, :]
            for part in range(2):
                rows = wind[part, level].astype(jnp.float32)
                first = 0 if at == 0 else 16 - SUB
                out[pl.ds((WIND + part * levels + level) * SUB, SUB), :] = rows[first : first + SUB]
        out[pl.ds(KD * SUB, SUB), :] = diffusion_of(wake[at : at + SUB, :])
        out[pl.ds(CHANNELS * SUB, 2), :] = jnp.zeros((2, out.shape[1]), jnp.float32)


def pack(inc, mult, winds, wake):
    levels, rows, columns = inc.shape
    field = [
        pl.BlockSpec((levels, 8, columns), lambda i, at=at: (0, at, 0))
        for at in (0, rows // 8 - 1)
    ]
    wind = [
        pl.BlockSpec((2, levels, 16, columns), lambda i, at=at: (0, 0, at, 0))
        for at in (0, rows // 16 - 1)
    ]
    mask = [pl.BlockSpec((8, columns), lambda i, at=at: (at, 0)) for at in (0, rows // 8 - 1)]
    message = f32(CHANNELS * SUB + 2, columns)
    return call(
        pack_kernel,
        [message, message],
        inc, inc, mult, mult, winds, winds, wake, wake,
        in_specs=field + field + wind + mask,
        grid=(1,),
    )


def scratch_of(levels, columns, rows=48):
    shape = (levels, columns // LANES, rows + 2 * BASE, LANES)
    return [pltpu.VMEM(shape, jnp.float32)] * 2 + [pltpu.VMEM((5,) + shape, jnp.float32)]


def centre_kernel(inc, winds, wake, out, a, b, coef, *, low, high):
    levels, rows, columns = inc.shape
    tiles = columns // LANES
    own_coeffs(coef, winds, wake, range(rows // 16), False)
    for level in range(levels):
        for j in range(tiles):
            a[level, j, pl.ds(BASE, rows), :] = inc[level, :, cols(j)]
    run_model(a, b, coef, [(low, high)], False)
    for level in range(levels):
        for j in range(tiles):
            out[level, :, cols(j)] = a[level, j, pl.ds(BASE + low, high - low), :]


def forward_centre(inc, winds, wake):
    levels, rows, columns = inc.shape
    low, high = EDGE, rows - EDGE
    return call(
        functools.partial(centre_kernel, low=low, high=high),
        f32(levels, high - low, columns),
        inc, winds, wake,
        scratch=scratch_of(levels, columns, rows),
    )


def edges_kernel(inc, winds, wake, above, below, out, rims, a, b, coef):
    levels, rows, columns = inc.shape
    tiles = columns // LANES
    own_coeffs(coef, winds, wake, (0, rows // 16 - 1), False)
    halo_coeffs(coef, above, BASE - SUB, levels, tiles, False)
    halo_coeffs(coef, below, BASE + rows, levels, tiles, False)
    for level in range(levels):
        part = pl.ds((INC + level) * SUB, SUB)
        rims[pl.ds(level * SUB, SUB), :] = above[pl.ds((MULT + level) * SUB, SUB), :]
        rims[pl.ds((levels + level) * SUB, SUB), :] = below[pl.ds((MULT + level) * SUB, SUB), :]
        for j in range(tiles):
            a[level, j, pl.ds(BASE, 16), :] = inc[level, :16, cols(j)]
            a[level, j, pl.ds(BASE + rows - 16, 16), :] = inc[level, rows - 16 :, cols(j)]
            a[level, j, pl.ds(BASE - SUB, SUB), :] = above[part, cols(j)]
            a[level, j, pl.ds(BASE + rows, SUB), :] = below[part, cols(j)]
    run_model(a, b, coef, [(0, EDGE), (rows - EDGE, rows)], False)
    for level in range(levels):
        for j in range(tiles):
            out[level, :EDGE, cols(j)] = a[level, j, pl.ds(BASE, EDGE), :]
            out[level, EDGE:, cols(j)] = a[level, j, pl.ds(BASE + rows - EDGE, EDGE), :]


def forward_edges(inc, winds, wake, above, below):
    levels, rows, columns = inc.shape
    return call(
        edges_kernel,
        [f32(levels, 2 * EDGE, columns), f32(2 * levels * SUB, columns)],
        inc, winds, wake, above, below,
        scratch=scratch_of(levels, columns, rows),
    )


def one_hots(cell, rows, columns):
    where = lax.broadcasted_iota(jnp.int32, (rows, LANES), 0) * columns
    offset = cell - where
    in_row = (offset >= 0) & (offset < columns)
    column = jnp.sum(jnp.where(in_row, offset, 0), axis=0, keepdims=True)
    in_column = lax.broadcasted_iota(jnp.int32, (columns, LANES), 0) == column
    return in_row, in_column.astype(jnp.float32)


def observe_kernel(inc, dual, var, cell, out, terms):
    levels, rows, columns = inc.shape
    in_row, in_column = one_hots(cell[...], levels * rows, columns)
    picked = jnp.dot(
        inc[...].reshape(levels * rows, columns),
        in_column,
        precision=lax.Precision.HIGHEST,
        preferred_element_type=jnp.float32,
    )
    sampled = jnp.sum(jnp.where(in_row, picked, 0.0), axis=0, keepdims=True)
    value = var[...] * dual[...] + sampled
    out[...] = value
    terms[...] = dual[...] * (value + sampled)


def observe(inc, dual, var, cell):
    shape = f32(*dual.shape)
    return call(observe_kernel, [shape, shape], inc, dual, var, cell)


def sums_kernel(mult, var, inc, incoming, centre, edges, terms, out):
    levels, rows, columns = inc.shape

    def part(moved, level, rows_at, row, total):
        here = pl.ds(row, 8)
        m, q = mult[level, here, :], inc[level, here, :]
        value = m * (var[level, here, :] * m + 2.0 * q)
        value -= 2.0 * (moved[level, pl.ds(rows_at, 8), :] * incoming[level, here, :])
        return total + value

    total = jnp.zeros((8, columns), jnp.float32)
    for level in range(levels):
        for at in range(0, EDGE, 8):
            total = part(edges, level, at, at, total)
            total = part(edges, level, EDGE + at, rows - EDGE + at, total)
        for at in range(0, rows - 2 * EDGE, 8):
            total = part(centre, level, at, EDGE + at, total)
    out[...] = jnp.full(out.shape, jnp.sum(total) + jnp.sum(terms[...]), jnp.float32)


def sums(count, mult, var, inc, incoming, centre, edges, terms):
    return call(sums_kernel, f32(count, LANES), mult, var, inc, incoming, centre, edges, terms)


def adjoint_kernel(
    incoming, rims, winds, wake, above, below, mult, dual, cell, out, a, b, coef
):
    levels, rows, columns = incoming.shape
    tiles = columns // LANES
    own_coeffs(coef, winds, wake, range(rows // 16), True)
    halo_coeffs(coef, above, BASE - SUB, levels, tiles, True)
    halo_coeffs(coef, below, BASE + rows, levels, tiles, True)
    for level in range(levels):
        for j in range(tiles):
            a[level, j, pl.ds(BASE, rows), :] = incoming[level, :, cols(j)]
            a[level, j, pl.ds(BASE - SUB, SUB), :] = rims[pl.ds(level * SUB, SUB), cols(j)]
            a[level, j, pl.ds(BASE + rows, SUB), :] = rims[
                pl.ds((levels + level) * SUB, SUB), cols(j)
            ]
    run_model(a, b, coef, [(0, rows)], True)
    in_row, in_column = one_hots(cell[...], levels * rows, columns)
    spread = lax.dot_general(
        jnp.where(in_row, dual[...], 0.0),
        in_column,
        (((1,), (1,)), ((), ())),
        precision=lax.Precision.HIGHEST,
        preferred_element_type=jnp.float32,
    )
    out[...] = mult[...] + spread.reshape(out.shape)
    for level in range(levels):
        for j in range(tiles):
            out[level, :, cols(j)] -= a[level, j, pl.ds(BASE, rows), :]


def adjoint(incoming, rims, winds, wake, above, below, mult, dual, cell):
    levels, rows, columns = incoming.shape
    return call(
        adjoint_kernel,
        f32(*incoming.shape),
        incoming, rims, winds, wake, above, below, mult, dual, cell,
        scratch=scratch_of(levels, columns, rows),
    )


def combine_kernel(var, mult, inc, centre, edges, out):
    rows = inc.shape[1]
    middle = pl.ds(EDGE, rows - 2 * EDGE)
    out[:, middle, :] = var[:, middle, :] * mult[:, middle, :] + (inc[:, middle, :] - centre[...])
    for here, there in ((pl.ds(0, EDGE), pl.ds(0, EDGE)), (pl.ds(rows - EDGE, EDGE), pl.ds(EDGE, EDGE))):
        out[:, here, :] = var[:, here, :] * mult[:, here, :] + (inc[:, here, :] - edges[:, there, :])


def combine(var, mult, inc, centre, edges):
    return call(combine_kernel, f32(*inc.shape), var, mult, inc, centre, edges)


def total_kernel(parts, out, *, scale):
    out[0, 0] = jnp.sum(parts[:, 0:1]) * scale


def after(value, *others):
    return lax.optimization_barrier((value, *others))[0]


def shards(multiplier, obs_dual, increment, error_var, obs_var, winds, wake, cell):
    mult, inc, var, wind = multiplier[0], increment[0], error_var[0], winds[0]
    windows, strips = lax.axis_size("tm"), lax.axis_size("tile")
    up = [(k, k + 1) for k in range(windows - 1)]
    down = [(k + 1, k) for k in range(windows - 1)]
    onward = [(t, t + 1) for t in range(strips - 1)]
    backward = [(t + 1, t) for t in range(strips - 1)]

    incoming = lax.ppermute(mult, "tm", down)
    centre = forward_centre(inc, wind, wake)
    centre_in = lax.ppermute(centre, "tm", up)
    top, bottom = pack(after(inc, centre), mult, wind, wake)
    above = lax.ppermute(bottom, "tile", onward)
    below = lax.ppermute(top, "tile", backward)
    out_obs, terms = observe(after(inc, top), obs_dual, obs_var, cell)
    edges, rims = forward_edges(inc, wind, wake, above, below)
    edges_in = lax.ppermute(edges, "tm", up)
    rims_in = lax.ppermute(rims, "tm", down)
    count = windows * strips
    partial = sums(count, mult, var, inc, incoming, centre, edges, terms)
    parts = lax.all_to_all(partial, ("tm", "tile"), 0, 0, tiled=True)
    out_inc = adjoint(incoming, rims_in, wind, wake, above, below, mult, obs_dual, cell)
    out_mult = combine(var, mult, inc, centre_in, edges_in)
    elements = count * (2 * inc.size + obs_dual.shape[1])
    curvature = jnp.sum(parts[:, 0]) / jnp.float32(elements)
    return out_mult[None], out_obs, out_inc[None], curvature


def solution(mesh):
    return jax.shard_map(
        shards,
        mesh=mesh,
        in_specs=(
            P("tm", None, "tile", None),
            P("tm", "tile"),
            P("tm", None, "tile", None),
            P("tm", None, "tile", None),
            P("tm", "tile"),
            P("tm", None, None, "tile", None),
            P("tile", None),
            P("tm", "tile"),
        ),
        out_specs=(P("tm", None, "tile", None), P("tm", "tile"), P("tm", None, "tile", None), P()),
        check_vma=False,
    )
```

```python
import functools

import jax
import jax.numpy as jnp
from jax import lax
from jax.experimental import pallas as pl
from jax.experimental.pallas import tpu as pltpu
from jax.sharding import PartitionSpec as P

SUB = 6
LANES = 128
KAPPA = 0.04
MIX = 0.05
BASE = 16
INC, WIND, KD, MULT = 0, 4, 12, 13
CHANNELS = 17
WEIGHTS = 5
MIB = 2**20
ANY = pl.BlockSpec(memory_space=pl.ANY)
VMEM = pl.BlockSpec(memory_space=pltpu.VMEM)


def call(body, out_shape, *args, scratch=(), vmem=16, flops=1000, **kwargs):
    return pl.pallas_call(
        body,
        out_shape=out_shape,
        scratch_shapes=list(scratch),
        compiler_params=pltpu.CompilerParams(vmem_limit_bytes=vmem * MIB),
        cost_estimate=pl.CostEstimate(flops=flops, bytes_accessed=1000, transcendentals=0),
        **kwargs,
    )(*args)


def in_hbm(*values):
    return [pltpu.with_memory_space_constraint(value, pltpu.HBM) for value in values]


def to_hbm(*shape):
    return pltpu.HBM(shape, jnp.float32)


def in_vmem(*shape):
    return pltpu.VMEM(shape, jnp.float32)


def f32(*shape):
    return jax.ShapeDtypeStruct(shape, jnp.float32)


def cols(j):
    return pl.ds(j * LANES, LANES)


def diffusion_of(wake):
    return KAPPA * (1.0 + 2.0 * wake.astype(jnp.float32))


def edge_lanes(rows):
    lane = lax.broadcasted_iota(jnp.int32, (rows, LANES), 1)
    return lane == 0, lane == LANES - 1, jnp.zeros((rows, LANES), jnp.float32)


def put_weights(coef, wind_at, kd_at, level, row, rows, transpose):
    columns = coef[0].shape[1]
    first, last, zero = edge_lanes(rows)

    def weights(j):
        u, v = wind_at(0, level, j), wind_at(1, level, j)
        kd = kd_at(j)
        south = kd - jnp.minimum(u, 0.0)
        east = kd - jnp.minimum(v, 0.0)
        return jnp.maximum(u, 0.0) + kd, south, jnp.maximum(v, 0.0) + kd, east

    here = pl.ds(row, rows)
    before, now = zero, weights(0)
    for j in range(columns):
        after = weights(j + 1) if j + 1 < columns else (zero,) * 4
        north, south, west, east = now
        coef[0][level, j, here, :] = (1.0 - 2.0 * MIX) - ((north + south) + (west + east))
        coef[1][level, j, here, :] = north
        coef[2][level, j, here, :] = south
        if transpose:
            coef[3][level, j, here, :] = pltpu.roll(jnp.where(last, before, east), 1, 1)
            coef[4][level, j, here, :] = pltpu.roll(jnp.where(first, after[2], west), LANES - 1, 1)
        else:
            coef[3][level, j, here, :] = west
            coef[4][level, j, here, :] = east
        before, now = east, after


FORWARD = ((0, 0), (1, 0), (2, 0), (3, 0), (4, 0))
TRANSPOSE = ((0, 0), (2, -1), (1, 1), (3, 0), (4, 0))


def strip_weights(coef, wind_v, wake_v, level, transpose):
    def rows_of(tile, carry):
        here = pl.ds(pl.multiple_of(tile * 16, 16), 16)
        put_weights(
            coef,
            lambda part, level, j: wind_v[part, level, here, cols(j)].astype(jnp.float32),
            lambda j: diffusion_of(wake_v[here, cols(j)]),
            level, BASE + tile * 16, 16, transpose,
        )
        return carry

    lax.fori_loop(0, wake_v.shape[0] // 16, rows_of, 0)


def halo_weights(coef, halo, level, row, transpose):
    levels = coef[0].shape[0]
    put_weights(
        coef,
        lambda part, level, j: halo[pl.ds((WIND + part * levels + level) * SUB, SUB), cols(j)],
        lambda j: halo[pl.ds(KD * SUB, SUB), cols(j)],
        level, row, SUB, transpose,
    )


def update(src, dst, coef, table, start, tiles):
    levels, columns = src.shape[0], src.shape[1]
    first, last, zero = edge_lanes(8)
    rows = [start + 8 * tile for tile in range(tiles)]
    blank = [[zero] * levels] * tiles

    def load(j):
        return [[src[level, j, pl.ds(row, 8), :] for level in range(levels)] for row in rows]

    before, now = blank, load(0)
    for j in range(columns):
        after = load(j + 1) if j + 1 < columns else blank
        for row, west, here, east in zip(rows, before, now, after):
            for level in range(levels):

                def weight(k):
                    which, shift = table[k]
                    return coef[which][level, j, pl.ds(row + shift, 8), :]

                middle = here[level]
                total = weight(0) * middle
                total += weight(1) * src[level, j, pl.ds(row - 1, 8), :]
                total += weight(2) * src[level, j, pl.ds(row + 1, 8), :]
                total += weight(3) * pltpu.roll(jnp.where(last, west[level], middle), 1, 1)
                total += weight(4) * pltpu.roll(jnp.where(first, east[level], middle), LANES - 1, 1)
                if level == 0:
                    vertical = here[1]
                elif level == levels - 1:
                    vertical = here[level - 1]
                else:
                    vertical = here[level - 1] + here[level + 1]
                dst[level, j, pl.ds(row, 8), :] = total + MIX * vertical
        before, now = now, after


def run_model(a, b, coef, table, rows):
    def tiles(reach):
        return -(-(rows + 2 * reach) // 8)

    update(a, b, coef, table, BASE - (SUB - 1), tiles(SUB - 1))

    def pair(i, carry):
        update(b, a, coef, table, BASE - (SUB - 2) + 2 * i, tiles(SUB - 2))
        update(a, b, coef, table, BASE - (SUB - 3) + 2 * i, tiles(SUB - 3))
        return carry

    lax.fori_loop(0, (SUB - 2) // 2, pair, 0)
    update(b, a, coef, table, BASE, tiles(0))


def pack_kernel(inc, mult, winds, wake, top, bottom, inc_v, mult_v, wind_v, wake_v, sems):
    levels, rows, columns = inc.shape
    copies = []
    for side, (row, row16) in enumerate(((0, 0), (rows - 8, rows - 16))):
        copies.append(
            [
                pltpu.make_async_copy(inc.at[:, pl.ds(row, 8), :], inc_v.at[side], sems.at[side, 0]),
                pltpu.make_async_copy(mult.at[:, pl.ds(row, 8), :], mult_v.at[side], sems.at[side, 1]),
                pltpu.make_async_copy(winds.at[:, :, pl.ds(row16, 16), :], wind_v.at[side], sems.at[side, 2]),
                pltpu.make_async_copy(wake.at[pl.ds(row, 8), :], wake_v.at[side], sems.at[side, 3]),
            ]
        )
    for copy in copies[0] + copies[1]:
        copy.start()
    for side, (out, at, at16) in enumerate(((top, 0, 0), (bottom, 8 - SUB, 16 - SUB))):
        for copy in copies[side]:
            copy.wait()
        for level in range(levels):
            out[pl.ds((INC + level) * SUB, SUB), :] = inc_v[side, level, at : at + SUB, :]
            out[pl.ds((MULT + level) * SUB, SUB), :] = mult_v[side, level, at : at + SUB, :]
            for part in range(2):
                wind = wind_v[side, part, level].astype(jnp.float32)
                out[pl.ds((WIND + part * levels + level) * SUB, SUB), :] = wind[at16 : at16 + SUB]
        out[pl.ds(KD * SUB, SUB), :] = diffusion_of(wake_v[side, at : at + SUB, :])
        out[pl.ds(CHANNELS * SUB, 2), :] = jnp.zeros((2, columns), jnp.float32)


def pack(inc, mult, winds, wake):
    levels, rows, columns = inc.shape
    message = in_vmem(CHANNELS * SUB + 2, columns)
    return call(
        pack_kernel,
        [message, message],
        *in_hbm(inc, mult, winds, wake),
        in_specs=[ANY] * 4,
        scratch=[
            pltpu.VMEM((2, levels, 8, columns), jnp.float32),
            pltpu.VMEM((2, levels, 8, columns), jnp.float32),
            pltpu.VMEM((2, 2, levels, 16, columns), jnp.bfloat16),
            pltpu.VMEM((2, 8, columns), jnp.int32),
            pltpu.SemaphoreType.DMA((2, 4)),
        ],
        vmem=6,
    )


def one_hots(cell, rows, columns):
    where = lax.broadcasted_iota(jnp.int32, (rows, LANES), 0) * columns
    offset = cell - where
    in_row = (offset >= 0) & (offset < columns)
    column = jnp.sum(jnp.where(in_row, offset, 0), axis=0, keepdims=True)
    in_column = lax.broadcasted_iota(jnp.int32, (columns, LANES), 0) == column
    return in_row, jnp.where(in_column, 1.0, 0.0).astype(jnp.bfloat16)


def three_parts(x):
    high = x.astype(jnp.bfloat16)
    rest = x - high.astype(jnp.float32)
    middle = rest.astype(jnp.bfloat16)
    return high, middle, (rest - middle.astype(jnp.float32)).astype(jnp.bfloat16)


def local_kernel(
    inc, mult, var, winds, wake, dual, obs_var, cell,
    out_obs, inc_base, mult_base, acc, field, *rest,
):
    coef, rest = rest[:WEIGHTS], rest[WEIGHTS:]
    inc_v, mult_v, var_v, wind_v, wake_v, in_sem, wind_sem, wake_sem, out_sem = rest
    levels, rows, columns = inc.shape
    tiles = columns // LANES
    wind_copies = [
        [pltpu.make_async_copy(winds.at[part, level], wind_v.at[part, level], wind_sem.at[part, level]) for part in range(2)]
        for level in range(levels)
    ]
    wake_copy = pltpu.make_async_copy(wake, wake_v, wake_sem)
    fetch = [
        [pltpu.make_async_copy(x.at[level], v.at[level], in_sem.at[k, level]) for level in range(levels)]
        for k, (x, v) in enumerate(((inc, inc_v), (mult, mult_v), (var, var_v)))
    ]
    wake_copy.start()
    for copy in [c for pair in wind_copies for c in pair] + [c for copies in fetch for c in copies]:
        copy.start()
    in_row, in_column = one_hots(cell[...], levels * rows, columns)
    spread = lax.dot_general(
        jnp.concatenate(three_parts(jnp.where(in_row, dual[...], 0.0)), axis=1),
        jnp.concatenate([in_column] * 3, axis=1),
        (((1,), (1,)), ((), ())),
        preferred_element_type=jnp.float32,
    )
    wake_copy.wait()
    for level in range(levels):
        for copy in wind_copies[level]:
            copy.wait()
        strip_weights(coef, wind_v, wake_v, level, False)
    for copy in fetch[0]:
        copy.wait()
    picked = jnp.zeros((levels * rows, LANES), jnp.float32)
    for part in three_parts(inc_v[...].reshape(levels * rows, columns)):
        picked += jnp.dot(part, in_column, preferred_element_type=jnp.float32)
    sampled = jnp.sum(jnp.where(in_row, picked, 0.0), axis=0, keepdims=True)
    value = obs_var[...] * dual[...] + sampled
    out_obs[...] = value
    total = jnp.zeros((8, columns), jnp.float32)
    results = []
    for level in range(levels):
        fetch[1][level].wait()
        fetch[2][level].wait()
        for row in range(0, rows, 8):
            here = pl.ds(row, 8)
            m, q = mult_v[level, here, :], inc_v[level, here, :]
            at = level * rows + row
            weighted = var_v[level, here, :] * m + q
            total += m * (weighted + q)
            mult_v[level, here, :] = m + spread[at : at + 8]
            var_v[level, here, :] = weighted
            for j in range(tiles):
                field[level, j, pl.ds(BASE + row, 8), :] = q[:, j * LANES : (j + 1) * LANES]
        for k, (v, x) in enumerate(((mult_v, inc_base), (var_v, mult_base))):
            results.append(pltpu.make_async_copy(v.at[level], x.at[level], out_sem.at[k, level]))
            results[-1].start()
    total = sum(total[:, j * LANES : (j + 1) * LANES] for j in range(tiles))
    first = lax.broadcasted_iota(jnp.int32, (8, LANES), 0) == 0
    acc[...] = total + jnp.where(first, dual[...] * (value + sampled), 0.0)
    for copy in results:
        copy.wait()


def local(inc, mult, var, winds, wake, dual, obs_var, cell):
    levels, rows, columns = inc.shape
    strip = to_hbm(levels, rows, columns)
    field = (levels, columns // LANES, rows + 2 * BASE, LANES)
    return call(
        local_kernel,
        [f32(*dual.shape), strip, strip, in_vmem(8, LANES)] + [in_vmem(*field)] * (1 + WEIGHTS),
        *in_hbm(inc, mult, var, winds, wake), dual, obs_var, cell,
        in_specs=[ANY] * 5 + [VMEM] * 3,
        out_specs=[VMEM, ANY, ANY] + [VMEM] * (2 + WEIGHTS),
        scratch=[pltpu.VMEM(inc.shape, jnp.float32)] * 3
        + [
            pltpu.VMEM(winds.shape, jnp.bfloat16),
            pltpu.VMEM(wake.shape, jnp.int32),
            pltpu.SemaphoreType.DMA((3, levels)),
            pltpu.SemaphoreType.DMA((2, levels)),
            pltpu.SemaphoreType.DMA,
            pltpu.SemaphoreType.DMA((2, levels)),
        ],
        vmem=12,
        flops=10**11,
    )


def forward_kernel(*refs):
    above, below, moved, rims, above_out, below_out, a = refs[1 + WEIGHTS : 8 + WEIGHTS]
    coef, (b, sems) = refs[8 + WEIGHTS : -2], refs[-2:]
    levels, rows, columns = moved.shape
    tiles = columns // LANES
    copies = [
        pltpu.make_async_copy(above, above_out, sems.at[0]),
        pltpu.make_async_copy(below, below_out, sems.at[1]),
    ]
    for copy in copies:
        copy.start()
    for halo, row, at in ((above, BASE - SUB, 0), (below, BASE + rows, levels)):
        for level in range(levels):
            halo_weights(coef, halo, level, row, False)
            rims[pl.ds((at + level) * SUB, SUB), :] = halo[pl.ds((MULT + level) * SUB, SUB), :]
            for j in range(tiles):
                a[level, j, pl.ds(row, SUB), :] = halo[pl.ds((INC + level) * SUB, SUB), cols(j)]
    run_model(a, b, coef, FORWARD, rows)
    for level in range(levels):
        for j in range(tiles):
            moved[level, :, cols(j)] = a[level, j, pl.ds(BASE, rows), :]
    for copy in copies:
        copy.wait()


def forward(field, coef, above, below, rows):
    levels, tiles = field.shape[:2]
    return call(
        forward_kernel,
        [
            in_vmem(levels, rows, tiles * LANES),
            in_vmem(2 * levels * SUB, tiles * LANES),
            to_hbm(*above.shape),
            to_hbm(*below.shape),
        ]
        + [in_vmem(*field.shape)] * (1 + WEIGHTS),
        field, *coef, above, below,
        in_specs=[VMEM] * (3 + WEIGHTS),
        out_specs=[VMEM, VMEM, ANY, ANY] + [VMEM] * (1 + WEIGHTS),
        input_output_aliases={i: i + 4 for i in range(1 + WEIGHTS)},
        scratch=[pltpu.VMEM(field.shape, jnp.float32), pltpu.SemaphoreType.DMA((2,))],
        vmem=4,
    )


def sums_kernel(moved, incoming, acc, out):
    levels, rows, columns = moved.shape
    total = jnp.zeros((8, columns), jnp.float32)
    for level in range(levels):
        for row in range(0, rows, 8):
            here = pl.ds(row, 8)
            total += moved[level, here, :] * incoming[level, here, :]
    total = sum(total[:, j * LANES : (j + 1) * LANES] for j in range(columns // LANES))
    out[...] = jnp.full(out.shape, jnp.sum(acc[...] - 2.0 * total), jnp.float32)


def sums(count, moved, incoming, acc):
    return call(sums_kernel, f32(count, LANES), moved, incoming, acc, vmem=6)


def adjoint_kernel(
    incoming, rims, inc_base, winds, wake, above, below, out,
    a, b, base_v, wind_v, wake_v, halo_v, wind_sem, base_sem, sems, *coef,
):
    levels, rows, columns = incoming.shape
    tiles = columns // LANES
    wake_copy = pltpu.make_async_copy(wake, wake_v, sems.at[0])
    winds_copies = [
        [pltpu.make_async_copy(winds.at[part, level], wind_v.at[part, level], wind_sem.at[part, level]) for part in range(2)]
        for level in range(levels)
    ]
    halos = [
        pltpu.make_async_copy(x, halo_v.at[k], sems.at[1 + k]) for k, x in enumerate((above, below))
    ]
    bases = [
        pltpu.make_async_copy(inc_base.at[level], base_v.at[level], base_sem.at[level])
        for level in range(levels)
    ]
    wake_copy.start()
    for copy in [c for pair in winds_copies for c in pair] + halos + bases:
        copy.start()
    for level in range(levels):
        for j in range(tiles):
            a[level, j, pl.ds(BASE, rows), :] = incoming[level, :, cols(j)]
            for row, at in ((BASE - SUB, level), (BASE + rows, levels + level)):
                a[level, j, pl.ds(row, SUB), :] = rims[pl.ds(at * SUB, SUB), cols(j)]
    wake_copy.wait()
    for level in range(levels):
        for copy in winds_copies[level]:
            copy.wait()
        strip_weights(coef, wind_v, wake_v, level, True)
    for copy in halos:
        copy.wait()
    for k, row in enumerate((BASE - SUB, BASE + rows)):
        for level in range(levels):
            halo_weights(coef, halo_v.at[k], level, row, True)
    run_model(a, b, coef, TRANSPOSE, rows)
    copies = []
    for level in range(levels):
        bases[level].wait()
        for j in range(tiles):
            base_v[level, :, cols(j)] -= a[level, j, pl.ds(BASE, rows), :]
        copies.append(pltpu.make_async_copy(base_v.at[level], out.at[level], base_sem.at[level]))
        copies[-1].start()
    for copy in copies:
        copy.wait()


def adjoint(incoming, rims, inc_base, winds, wake, above, below):
    levels, rows, columns = incoming.shape
    field = (levels, columns // LANES, rows + 2 * BASE, LANES)
    return call(
        adjoint_kernel,
        to_hbm(*incoming.shape),
        incoming, rims, *in_hbm(inc_base, winds, wake, above, below),
        in_specs=[VMEM] * 2 + [ANY] * 5,
        out_specs=ANY,
        scratch=[
            pltpu.VMEM(field, jnp.float32),
            pltpu.VMEM(field, jnp.float32),
            pltpu.VMEM(incoming.shape, jnp.float32),
            pltpu.VMEM(winds.shape, jnp.bfloat16),
            pltpu.VMEM(wake.shape, jnp.int32),
            pltpu.VMEM((2,) + above.shape, jnp.float32),
            pltpu.SemaphoreType.DMA((2, levels)),
            pltpu.SemaphoreType.DMA((levels,)),
            pltpu.SemaphoreType.DMA((3,)),
        ]
        + [pltpu.VMEM(field, jnp.float32)] * WEIGHTS,
        vmem=28,
    )


def finish_kernel(base, moved, parts, out, curvature, base_v, parts_v, sems, *, elements):
    levels = base.shape[0]
    fetch = [
        pltpu.make_async_copy(base.at[level], base_v.at[level], sems.at[level])
        for level in range(levels)
    ]
    fetch_parts = pltpu.make_async_copy(parts, parts_v, sems.at[levels])
    for copy in fetch + [fetch_parts]:
        copy.start()
    copies = []
    for level in range(levels):
        fetch[level].wait()
        base_v[level] -= moved[level]
        copies.append(pltpu.make_async_copy(base_v.at[level], out.at[level], sems.at[level]))
        copies[-1].start()
    fetch_parts.wait()
    total = jnp.sum(parts_v[...], axis=0, keepdims=True)[:, :1]
    curvature[...] = total / jnp.float32(elements)
    for copy in copies:
        copy.wait()


def finish(base, moved, parts, elements):
    levels = base.shape[0]
    base, parts = in_hbm(base, parts)
    return call(
        functools.partial(finish_kernel, elements=elements),
        [to_hbm(*base.shape), f32(1, 1)],
        base, moved, parts,
        in_specs=[ANY, VMEM, ANY],
        out_specs=[ANY, VMEM],
        scratch=[
            pltpu.VMEM(base.shape, jnp.float32),
            pltpu.VMEM(parts.shape, jnp.float32),
            pltpu.SemaphoreType.DMA((levels + 1,)),
        ],
        vmem=6,
    )


def shards(multiplier, obs_dual, increment, error_var, obs_var, winds, wake, cell):
    mult, inc, var, wind = multiplier[0], increment[0], error_var[0], winds[0]
    windows, strips = lax.axis_size("tm"), lax.axis_size("tile")
    count = windows * strips
    up = [(k, k + 1) for k in range(windows - 1)]
    down = [(k + 1, k) for k in range(windows - 1)]
    onward = [(t, t + 1) for t in range(strips - 1)]
    backward = [(t + 1, t) for t in range(strips - 1)]

    incoming = lax.ppermute(mult, "tm", down)
    top, bottom = pack(inc, mult, wind, wake)
    above = lax.ppermute(bottom, "tile", onward)
    below = lax.ppermute(top, "tile", backward)
    inc, top = lax.optimization_barrier((inc, top))
    out_obs, inc_base, mult_base, acc, field, *coef = local(
        inc, mult, var, wind, wake, obs_dual, obs_var, cell
    )
    moved, rims, above, below, *_ = forward(field, coef, above, below, inc.shape[1])
    moved_in = lax.ppermute(moved, "tm", up)
    rims_in = lax.ppermute(rims, "tm", down)
    partial = sums(count, moved, incoming, acc)
    parts = lax.all_to_all(partial, ("tm", "tile"), 0, 0, tiled=True)
    out_inc = adjoint(incoming, rims_in, inc_base, wind, wake, above, below)
    elements = count * (2 * inc.size + obs_dual.shape[1])
    out_mult, curvature = finish(mult_base, moved_in, parts, elements)
    return out_mult[None], out_obs, out_inc[None], curvature[0, 0]


def solution(mesh):
    return jax.shard_map(
        shards,
        mesh=mesh,
        in_specs=(
            P("tm", None, "tile", None),
            P("tm", "tile"),
            P("tm", None, "tile", None),
            P("tm", None, "tile", None),
            P("tm", "tile"),
            P("tm", None, None, "tile", None),
            P("tile", None),
            P("tm", "tile"),
        ),
        out_specs=(P("tm", None, "tile", None), P("tm", "tile"), P("tm", None, "tile", None), P()),
        check_vma=False,
    )
```
